32 devices in a mesh: grp: 2 (over x), inp: 4 (over y, core), tm: 4 (over z).
Axes of the slice: x: 2, y: 2, z: 4, core: 2. Of those that a mesh axis runs over, the one named last changes fastest.
Arguments:
- samples: bfloat16 [64, 1024, 8192], P(('grp', 'tm'), 'inp'), parts along dimension 0, may hold values from -6 to 6
- fir: float32 [16, 8192], replicated, may hold values from -1 to 1
- flags: int32 [64, 1024], P(('grp', 'tm'), 'inp'), parts along dimension 0, may hold values 0 or 1
Outputs:
- visibilities: float32 [16, 2, 1024, 1024], P(('grp', 'tm'), None, 'inp'), parts along dimension 0
The draws below stay inside these ranges and needn't reach their ends.
There are 2 independent parts, one for each index of `grp`. The reference program is written for one: setup_inputs(seed, part) draws one part's arguments, and reference() takes and returns one part's arrays. A program takes and returns all parts, laid end to end along the dimension named above; an argument that names none is the same for every part. Nothing has to cross between parts.
All inputs are finite; a program needn't handle non-finite values. No bound on the sum of `flags` on one device may be relied on, other than what follows from the above.
Results may differ from the reference program's by a relative error of at most 0.0063.
Values may be sent and summed in bfloat16 or wider, within the bound.
No kernel may reach another device: no remote copies, remote signals or barrier semaphores. Data moves between devices by JAX's collectives and lax.ppermute only.
A program may use at most 256 MiB of HBM per device.

```python
import math
import jax
import jax.numpy as jnp
from jax import lax

NI = 1024
NCH = 4096
LEN = 8192
TAPS = 16
SPEC_DEV = 8
NSPEC = 32
CB = 8
HOPS = 2


def touch_ends(values, rng, least, high):
    place = [jax.random.randint(jax.random.fold_in(rng, axis), (), 0, length) for axis, length in enumerate(values.shape)]
    widest = values.shape.index(max(values.shape))
    next_to = place[:widest] + [(place[widest] + 1) % values.shape[widest]] + place[widest + 1:]
    return values.at[tuple(place)].set(least).at[tuple(next_to)].set(high)


def level_of(rng, extent, pieces, smallest, high):
    loudness, own = 1.0, jax.random.fold_in(rng, 6)
    for dim, parts in pieces:
        steps = jnp.exp(jax.random.uniform(jax.random.fold_in(own, dim), (parts,), jnp.float32, smallest / len(pieces), high / len(pieces)))
        loudness = loudness * jnp.repeat(steps, extent[dim] // parts).reshape([-1 if axis == dim else 1 for axis in range(len(extent))])
    return loudness


def noise(rng, shape, spread, limit, pieces=(), kind=jnp.bfloat16):
    values = jax.random.normal(rng, shape, jnp.float32) * spread
    if len(pieces) > 0:
        values = level_of(rng, shape, pieces, -0.22, 0.18) * values
    return jnp.clip(values, min=-limit, max=limit).astype(kind)


def setup_inputs(seed: int = 0, part: int = 0) -> dict:
    splits = jax.random.split(jax.random.key(seed), 4)
    part_keys = jax.random.split(jax.random.fold_in(splits[3], part), 4)
    return {
        "samples": noise(part_keys[0], (NSPEC, NI, LEN), 1.0, 6.0, ((0, 4), (1, 4))),
        "fir": noise(splits[1], (TAPS, LEN), 0.25, 1.0, (), jnp.float32),
        "flags": touch_ends((jax.random.randint(part_keys[2], (NSPEC, NI), 0, 8) < 7).astype(jnp.int32), jax.random.fold_in(part_keys[2], 1), 0, 1),
    }


def band_table(length, count, lowest):
    sample_ids = jnp.arange(length, dtype=jnp.int32)
    channel_ids = lowest + jnp.arange(count, dtype=jnp.int32)
    phase = sample_ids[:, None] * channel_ids[None, :] % length
    angle = 2.0 * math.pi / length * phase.astype(jnp.float32)
    factor = math.sqrt(2.0 / length)
    both = jnp.concatenate([factor * jnp.cos(angle), -factor * jnp.sin(angle)], axis=1)
    return both.astype(jnp.bfloat16)

def reference(samples, fir, flags):
    block = min(NI, 128)
    table = band_table(LEN, CB, NCH // 4).astype(jnp.float32)
    frame_ids = jnp.arange(NSPEC, dtype=jnp.int32)
    own_block = frame_ids // SPEC_DEV

    def channelize(block_index):
        first = (block_index * block).astype(jnp.int32)
        frames = lax.dynamic_slice_in_dim(samples, first, block, 1)
        padded = jnp.concatenate([jnp.zeros((TAPS - 1, block, LEN), samples.dtype), frames], axis=0)
        band = jnp.zeros((NSPEC, block, 2 * CB), jnp.float32)
        for hop in range(HOPS + 1):
            filtered = jnp.zeros((NSPEC, block, LEN), jnp.float32)
            for tap_index in range(TAPS):
                source = frame_ids - TAPS + 1 + tap_index
                source_block = jnp.floor_divide(source, SPEC_DEV)
                keep = (own_block - source_block == hop).astype(jnp.float32)
                filtered = filtered + keep[:, None, None] * fir[tap_index][None, None, :] * padded[tap_index:tap_index + NSPEC].astype(jnp.float32)
            part = filtered.astype(jnp.bfloat16).astype(jnp.float32)
            band = band + jnp.einsum('kbl,lq->kbq', part, table, precision=lax.Precision.HIGHEST)
        good = lax.dynamic_slice_in_dim(flags, first, block, 1).astype(jnp.float32)
        return (band * good[:, :, None]).astype(jnp.bfloat16)
    blocks = lax.map(channelize, jnp.arange(NI // block, dtype=jnp.int32))
    spectra = jnp.transpose(blocks, (1, 0, 2, 3)).reshape(NSPEC, NI, 2, CB)
    spectra = jnp.transpose(spectra, (0, 2, 3, 1))

    def correlate(channel):
        column = lax.dynamic_index_in_dim(spectra, channel, 2, keepdims=False).astype(jnp.float32)
        rotated = jnp.stack([-column[:, 1], column[:, 0]], axis=1)
        real = jnp.einsum('kpi,kpj->ij', column, column, precision=lax.Precision.HIGHEST)
        imag = jnp.einsum('kpi,kpj->ij', column, rotated, precision=lax.Precision.HIGHEST)
        return jnp.stack([real, imag], axis=0) / NSPEC
    return lax.map(correlate, jnp.arange(CB, dtype=jnp.int32))
```

```python
import functools

import jax
import jax.numpy as jnp
import ml_dtypes
import numpy as np
from jax import lax
from jax.experimental import pallas as pl
from jax.experimental.pallas import tpu as pltpu
from jax.sharding import PartitionSpec as P

NCH = 4096
CH_DEV = 2
SUBLANES = 8
LANES = 128
ROW_TILE = 16
FLAGGED = 1e30
MIB = 1 << 20


def round_up(value, step):
    return -(-value // step) * step


def partner(index, distance, count):
    if count & (count - 1) == 0:
        return index ^ distance
    return (distance - index) % count


def exchange(value, axis, distance):
    count = lax.axis_size(axis)
    return lax.ppermute(value, axis, [(source, partner(source, distance, count)) for source in range(count)])


def slab_table(length, slabs, lowest):
    sample_ids = np.arange(length, dtype=np.int64)
    channel_ids = lowest + np.arange(slabs * CH_DEV, dtype=np.int64)
    angle = 2.0 * np.pi / length * (channel_ids[:, None] * sample_ids[None, :] % length)
    factor = np.sqrt(2.0 / length)
    both = np.stack([factor * np.cos(angle), -factor * np.sin(angle)], axis=0)
    by_slab = both.reshape(2, slabs, CH_DEV, length).transpose(1, 0, 2, 3).reshape(slabs, 2 * CH_DEV, length)
    return np.tile(by_slab, (1, SUBLANES // (2 * CH_DEV), 1)).astype(ml_dtypes.bfloat16)


def channelize(slabs, window, me_ref, samples_ref, fir_ref, table_ref, flags_ref, *rest):
    outs, (weights, sums, total) = rest[:slabs], rest[slabs:]
    step = pl.program_id(0)
    frames, inputs, width = samples_ref.shape
    taps = fir_ref.shape[0]
    group = 2 * CH_DEV
    per_slab = taps * group
    pack = SUBLANES // group
    row_ids = lax.broadcasted_iota(jnp.int32, (SUBLANES, width), 0)

    @pl.when(step == 0)
    def _():
        sums[...] = jnp.zeros_like(sums)

    tables = [table_ref[partner(me_ref[0], slot, slabs)].astype(jnp.float32) for slot in range(slabs)]
    for first in range(0, taps, 2 * pack):
        coefs = []
        for half in range(2):
            coef = None
            for place in range(pack):
                tap = taps - 1 - (first + half * pack + place)
                line = jnp.broadcast_to(fir_ref[tap : tap + 1, :], (SUBLANES, width))
                coef = line if coef is None else jnp.where(row_ids >= place * group, line, coef)
            coefs.append(coef)
        for slot in range(slabs):
            rows = jnp.concatenate([coef * tables[slot] for coef in coefs], axis=0)
            weights[pl.ds(slot * per_slab + first * group, ROW_TILE), :] = rows.astype(jnp.bfloat16)

    for frame in range(frames):
        sums[frame] += lax.dot_general(
            weights[...], samples_ref[frame], (((1,), (1,)), ((), ())), preferred_element_type=jnp.float32
        )

    @pl.when(step == pl.num_programs(0) - 1)
    def _():
        for slot in range(slabs):
            total[...] = jnp.zeros_like(total)
            for frame in range(frames):
                total[pl.ds(frame * group, per_slab), :] += sums[frame, pl.ds(slot * per_slab, per_slab), :]
            good = jnp.broadcast_to(flags_ref[...][:, None, :], (frames, group, inputs)).reshape(frames * group, inputs)
            own = frames * group
            total[0:own, :] = jnp.where(good == 0, FLAGGED, total[0:own, :])
            outs[slot][...] = total[...].astype(outs[slot].dtype)


def add_hops(slabs, frames, me_ref, *rest):
    pieces, (out_ref, total) = rest[:slabs], rest[slabs:]
    group = 2 * CH_DEV
    total[...] = jnp.zeros_like(total)
    for slot in range(slabs):
        place = pl.multiple_of(partner(me_ref[0], slot, slabs) * (frames * group), SUBLANES)
        total[pl.ds(place, pieces[slot].shape[0]), :] += pieces[slot][...].astype(jnp.float32)
    value = total[0 : out_ref.shape[0], :]
    out_ref[...] = jnp.where(value > 0.5 * FLAGGED, 0.0, value).astype(out_ref.dtype)


def correlate(scale, me_ref, own_ref, *rest):
    pieces, (out_ref, left) = rest[:-2], rest[-2:]
    step = pl.program_id(0)
    rows, inputs = own_ref.shape
    group = 2 * CH_DEV

    @pl.when(step == 0)
    def _():
        own = own_ref[...].astype(jnp.float32)
        row_ids = lax.broadcasted_iota(jnp.int32, own.shape, 0)
        is_real = row_ids % group < CH_DEV
        turned = jnp.where(is_real, pltpu.roll(own, rows - CH_DEV, 0), -pltpu.roll(own, CH_DEV, 0))
        for channel in range(CH_DEV):
            keep = row_ids % CH_DEV == channel
            for part, value in enumerate((own, turned)):
                place = (channel * 2 + part) * inputs
                left[pl.ds(place, inputs), :] = jnp.where(keep, value, 0.0).T.astype(left.dtype)

    for slot, piece in enumerate(pieces):
        @pl.when(step == slot)
        def _(piece=piece):
            product = jnp.dot(left[...], piece[...], preferred_element_type=jnp.float32)
            out_ref[...] = (product * scale).reshape(out_ref.shape)


def shards(samples, fir, flags):
    frames, inputs, length = samples.shape
    taps = fir.shape[0]
    slabs = lax.axis_size("tm")
    blocks = lax.axis_size("inp")
    group = 2 * CH_DEV
    window = frames + taps - 1
    rows = round_up(window * group, ROW_TILE)
    spectra_rows = slabs * frames * group
    width = min(length, 1024)
    table = jnp.asarray(slab_table(length, slabs, NCH // 4))
    my_slab = lax.axis_index("tm").astype(jnp.int32).reshape(1)
    my_block = lax.axis_index("inp").astype(jnp.int32).reshape(1)

    sent = pl.pallas_call(
        functools.partial(channelize, slabs, window),
        grid_spec=pltpu.PrefetchScalarGridSpec(
            num_scalar_prefetch=1,
            grid=(length // width,),
            in_specs=[
                pl.BlockSpec((frames, inputs, width), lambda step, me: (0, 0, step)),
                pl.BlockSpec((taps, width), lambda step, me: (0, step)),
                pl.BlockSpec((slabs, SUBLANES, width), lambda step, me: (0, 0, step)),
                pl.BlockSpec((frames, inputs), lambda step, me: (0, 0)),
            ],
            out_specs=[pl.BlockSpec((rows, inputs), lambda step, me: (0, 0))] * slabs,
            scratch_shapes=[
                pltpu.VMEM((slabs * taps * group, width), jnp.bfloat16),
                pltpu.VMEM((frames, slabs * taps * group, inputs), jnp.float32),
                pltpu.VMEM((rows, inputs), jnp.float32),
            ],
        ),
        out_shape=[
            jax.ShapeDtypeStruct((rows, inputs), jnp.bfloat16 if slot else jnp.float32) for slot in range(slabs)
        ],
        compiler_params=pltpu.CompilerParams(vmem_limit_bytes=32 * MIB),
        name="channelize",
    )(my_slab, samples, fir, table, flags)

    pieces = [sent[0]] + [exchange(sent[slot], "tm", slot) for slot in range(1, slabs)]
    spectra = pl.pallas_call(
        functools.partial(add_hops, slabs, frames),
        grid_spec=pltpu.PrefetchScalarGridSpec(
            num_scalar_prefetch=1,
            grid=(1,),
            in_specs=[pl.BlockSpec((rows, inputs), lambda step, me: (0, 0))] * slabs,
            out_specs=pl.BlockSpec((spectra_rows, inputs), lambda step, me: (0, 0)),
            scratch_shapes=[pltpu.VMEM((spectra_rows + rows, inputs), jnp.float32)],
        ),
        out_shape=jax.ShapeDtypeStruct((spectra_rows, inputs), jnp.bfloat16),
        name="add_hops",
    )(my_slab, *pieces)

    if inputs % LANES == 0:
        gathered = [spectra] + [exchange(spectra, "inp", slot) for slot in range(1, blocks)]
    else:
        gathered = [lax.all_gather(spectra, "inp", axis=1, tiled=True)]
    columns = gathered[0].shape[1]
    return pl.pallas_call(
        functools.partial(correlate, 1.0 / (slabs * frames)),
        grid_spec=pltpu.PrefetchScalarGridSpec(
            num_scalar_prefetch=1,
            grid=(len(gathered),),
            in_specs=[pl.BlockSpec((spectra_rows, inputs), lambda step, me: (0, 0))]
            + [pl.BlockSpec((spectra_rows, columns), lambda step, me: (0, 0))] * len(gathered),
            out_specs=pl.BlockSpec(
                (CH_DEV, 2, inputs, columns),
                lambda step, me: (0, 0, 0, partner(me[0], step, blocks) if len(gathered) > 1 else 0),
            ),
            scratch_shapes=[pltpu.VMEM((CH_DEV * 2 * inputs, spectra_rows), jnp.bfloat16)],
        ),
        out_shape=jax.ShapeDtypeStruct((CH_DEV, 2, inputs, blocks * inputs), jnp.float32),
        name="correlate",
    )(my_block, spectra, *gathered)


def solution(mesh):
    in_specs = (P(("grp", "tm"), "inp", None), P(), P(("grp", "tm"), "inp"))
    out_specs = P(("grp", "tm"), None, "inp", None)
    return jax.shard_map(shards, mesh=mesh, in_specs=in_specs, out_specs=out_specs, check_vma=False)
```

```python
import functools

import jax
import jax.numpy as jnp
import ml_dtypes
import numpy as np
from jax import lax
from jax.experimental import pallas as pl
from jax.experimental.pallas import tpu as pltpu
from jax.sharding import PartitionSpec as P

NCH = 4096
CH_DEV = 2
SUBLANES = 8
LANES = 128
CORES = 2
ROW_TILE = 16
FLAGGED = 1e30
MIB = 1 << 20
WIDTH = 1024
AHEAD = 2


def round_up(value, step):
    return -(-value // step) * step


def partner(index, distance, count):
    if count & (count - 1) == 0:
        return index ^ distance
    return (distance - index) % count


def exchange(value, axis, distance):
    count = lax.axis_size(axis)
    return lax.ppermute(value, axis, [(source, partner(source, distance, count)) for source in range(count)])


def slab_table(length, slabs, lowest):
    sample_ids = np.arange(length, dtype=np.int64)
    channel_ids = lowest + np.arange(slabs * CH_DEV, dtype=np.int64)
    angle = 2.0 * np.pi / length * (channel_ids[:, None] * sample_ids[None, :] % length)
    factor = np.sqrt(2.0 / length)
    both = np.stack([factor * np.cos(angle), -factor * np.sin(angle)], axis=0)
    by_slab = both.reshape(2, slabs, CH_DEV, length).transpose(1, 0, 2, 3).reshape(slabs, 2 * CH_DEV, length)
    return np.tile(by_slab, (1, SUBLANES // (2 * CH_DEV), 1)).astype(ml_dtypes.bfloat16)


def cut(length):
    widths = [WIDTH // 2] + [WIDTH] * (length // WIDTH - 1) + [WIDTH // 2] if length % WIDTH == 0 else [length]
    starts = np.cumsum([0] + widths)
    return [(int(start), width) for start, width in zip(starts, widths)]


def channelize(slabs, me_ref, samples_hbm, fir_hbm, table_hbm, flags_hbm, *rest):
    outs, (samples, fir, table, flags, weights, sums, total, chunk_sems, sems) = rest[:slabs], rest[slabs:]
    frames, inputs, length = samples.shape
    taps = fir.shape[0]
    group = 2 * CH_DEV
    per_slab = taps * group
    pack = SUBLANES // group
    chunks = cut(length)
    small = [
        pltpu.make_async_copy(source, target, sems.at[place])
        for place, (source, target) in enumerate(((fir_hbm, fir), (table_hbm, table), (flags_hbm, flags)))
    ]
    loads = [
        pltpu.make_async_copy(
            samples_hbm.at[:, :, pl.ds(start, width)], samples.at[:, :, pl.ds(start, width)], chunk_sems.at[place]
        )
        for place, (start, width) in enumerate(chunks)
    ]
    for copy in small + loads[:AHEAD]:
        copy.start()

    def make_weights(start, width):
        row_ids = lax.broadcasted_iota(jnp.int32, (SUBLANES, width), 0)
        columns = pl.ds(start, width)
        tables = [table[partner(me_ref[0], slot, slabs), :, columns].astype(jnp.float32) for slot in range(slabs)]
        for first in range(0, taps, 2 * pack):
            coefs = []
            for half in range(2):
                coef = None
                for place in range(pack):
                    tap = taps - 1 - (first + half * pack + place)
                    line = jnp.broadcast_to(fir[tap : tap + 1, columns], (SUBLANES, width))
                    coef = line if coef is None else jnp.where(row_ids >= place * group, line, coef)
                coefs.append(coef)
            for slot in range(slabs):
                rows = jnp.concatenate([coef * tables[slot] for coef in coefs], axis=0)
                weights[pl.ds(slot * per_slab + first * group, ROW_TILE), columns] = rows.astype(jnp.bfloat16)

    total[...] = jnp.zeros_like(total)
    for copy in small:
        copy.wait()
    for copy in loads[AHEAD:]:
        copy.start()
    make_weights(*chunks[0])
    for place, (start, width) in enumerate(chunks):
        loads[place].wait()
        columns = pl.ds(start, width)
        if place + 1 < len(chunks):
            make_weights(*chunks[place + 1])
        for frame in range(frames):
            before = sums[frame] if place else jnp.zeros(sums.shape[1:], jnp.float32)
            after = before + lax.dot_general(
                weights[:, columns],
                samples[frame, :, columns],
                (((1,), (1,)), ((), ())),
                preferred_element_type=jnp.float32,
            )
            if place + 1 < len(chunks):
                sums[frame] = after
                continue
            for slot in range(slabs):
                total[slot, pl.ds(frame * group, per_slab), :] += after[slot * per_slab : (slot + 1) * per_slab]

    good = jnp.broadcast_to(flags[...][:, None, :], (frames, group, inputs)).reshape(frames * group, inputs)
    own = frames * group
    for slot in range(slabs):
        total[slot, 0:own, :] = jnp.where(good == 0, FLAGGED, total[slot, 0:own, :])
        outs[slot][...] = total[slot].astype(outs[slot].dtype)


def add_hops(slabs, frames, me_ref, *rest):
    pieces, (out_ref, total) = rest[:slabs][::-1], rest[slabs:]
    group = 2 * CH_DEV
    total[...] = jnp.zeros_like(total)
    for slot in range(slabs):
        place = pl.multiple_of(partner(me_ref[0], slot, slabs) * (frames * group), SUBLANES)
        total[pl.ds(place, pieces[slot].shape[0]), :] += pieces[slot][...].astype(jnp.float32)
    value = total[0 : out_ref.shape[0], :]
    out_ref[...] = jnp.where(value > 0.5 * FLAGGED, 0.0, value).astype(out_ref.dtype)


def make_left(own_ref, left_ref):
    rows, inputs = own_ref.shape
    group = 2 * CH_DEV
    own = own_ref[...].astype(jnp.float32)
    row_ids = lax.broadcasted_iota(jnp.int32, own.shape, 0)
    is_real = row_ids % group < CH_DEV
    turned = jnp.where(is_real, pltpu.roll(own, rows - CH_DEV, 0), -pltpu.roll(own, CH_DEV, 0))
    for channel in range(CH_DEV):
        keep = row_ids % CH_DEV == channel
        for part, value in enumerate((own, turned)):
            place = (channel * 2 + part) * inputs
            left_ref[pl.ds(place, inputs), :] = jnp.where(keep, value, 0.0).T.astype(left_ref.dtype)


def multiply(scale, blocks, slots, me_ref, left_ref, pieces, out_hbm, parts, sems):
    copies = []
    inputs = parts.shape[3]
    for place, (slot, piece) in enumerate(zip(slots, pieces)):
        width = piece.shape[1]
        first = 0 if blocks == 1 else pl.multiple_of(partner(me_ref[0], slot, blocks) * width, LANES)
        for channel in range(CH_DEV):
            for part in range(2):
                rows = left_ref[pl.ds((channel * 2 + part) * inputs, inputs), :]
                parts[place, channel, part] = jnp.dot(rows, piece[...], preferred_element_type=jnp.float32) * scale
                copies.append(
                    pltpu.make_async_copy(
                        parts.at[place, channel, part],
                        out_hbm.at[channel, part, :, pl.ds(first, width)],
                        sems.at[place, channel, part],
                    )
                )
                copies[-1].start()
    for copy in copies:
        copy.wait()


def correlate_first(scale, blocks, slots, me_ref, own_ref, *rest):
    pieces, (out_hbm, left_ref, parts, sems) = rest[: len(slots)], rest[len(slots) :]
    make_left(own_ref, left_ref)
    multiply(scale, blocks, slots, me_ref, left_ref, pieces, out_hbm, parts, sems)


def correlate_rest(scale, blocks, slots, me_ref, left_ref, *rest):
    pieces, (_, out_hbm, parts, sems) = rest[: len(slots)], rest[len(slots) :]
    multiply(scale, blocks, slots, me_ref, left_ref, pieces, out_hbm, parts, sems)


def shards(samples, fir, flags):
    frames, inputs, length = samples.shape
    taps = fir.shape[0]
    slabs = lax.axis_size("tm")
    blocks = lax.axis_size("inp")
    group = 2 * CH_DEV
    window = frames + taps - 1
    rows = round_up(window * group, ROW_TILE)
    spectra_rows = slabs * frames * group
    table = jnp.asarray(slab_table(length, slabs, NCH // 4))
    my_slab = lax.axis_index("tm").astype(jnp.int32).reshape(1)
    my_block = lax.axis_index("inp").astype(jnp.int32).reshape(1)

    chunks = len(cut(length))
    sent = pl.pallas_call(
        functools.partial(channelize, slabs),
        in_specs=[pl.BlockSpec(memory_space=pltpu.SMEM)] + [pl.BlockSpec(memory_space=pltpu.HBM)] * 4,
        out_specs=[pl.BlockSpec(memory_space=pltpu.VMEM)] * slabs,
        scratch_shapes=[
            pltpu.VMEM(samples.shape, samples.dtype),
            pltpu.VMEM(fir.shape, fir.dtype),
            pltpu.VMEM(table.shape, table.dtype),
            pltpu.VMEM(flags.shape, flags.dtype),
            pltpu.VMEM((slabs * taps * group, length), jnp.bfloat16),
            pltpu.VMEM((frames, slabs * taps * group, inputs), jnp.float32),
            pltpu.VMEM((slabs, rows, inputs), jnp.float32),
            pltpu.SemaphoreType.DMA((chunks,)),
            pltpu.SemaphoreType.DMA((3,)),
        ],
        out_shape=[
            jax.ShapeDtypeStruct((rows, inputs), jnp.bfloat16 if slot else jnp.float32) for slot in range(slabs)
        ],
        compiler_params=pltpu.CompilerParams(vmem_limit_bytes=56 * MIB),
        name="channelize",
    )(my_slab, samples, fir, table, flags)

    arrived = {slot: exchange(sent[slot], "tm", slot) for slot in reversed(range(1, slabs))}
    pieces = [jnp.maximum(sent[0], -FLAGGED)] + [arrived[slot] for slot in range(1, slabs)]
    smem = pl.BlockSpec(memory_space=pltpu.SMEM)
    vmem = pl.BlockSpec(memory_space=pltpu.VMEM)
    hbm = pl.BlockSpec(memory_space=pltpu.HBM)
    spectra = pl.pallas_call(
        functools.partial(add_hops, slabs, frames),
        in_specs=[smem] + [vmem] * slabs,
        out_specs=vmem,
        scratch_shapes=[pltpu.VMEM((spectra_rows + rows, inputs), jnp.float32)],
        out_shape=jax.ShapeDtypeStruct((spectra_rows, inputs), jnp.bfloat16),
        compiler_params=pltpu.CompilerParams(vmem_limit_bytes=4 * MIB),
        name="add_hops",
    )(my_slab, *pieces[::-1])

    scale = 1.0 / (slabs * frames)
    out_shape = jax.ShapeDtypeStruct((CH_DEV, 2, inputs, blocks * inputs), jnp.float32)
    left_shape = jax.ShapeDtypeStruct((CH_DEV * 2 * inputs, spectra_rows), jnp.bfloat16)

    def scratch(count, width):
        return [pltpu.VMEM((count, CH_DEV, 2, inputs, width), jnp.float32), pltpu.SemaphoreType.DMA((count, CH_DEV, 2))]

    if inputs % LANES:
        columns = lax.all_gather(spectra, "inp", axis=1, tiled=True)
        return pl.pallas_call(
            functools.partial(correlate_first, scale, 1, (0,)),
            in_specs=[smem, vmem, vmem],
            out_specs=[hbm, vmem],
            out_shape=[out_shape, left_shape],
            scratch_shapes=scratch(1, blocks * inputs),
            compiler_params=pltpu.CompilerParams(vmem_limit_bytes=16 * MIB),
        name="correlate",
        )(my_block, spectra, columns)[0]

    slots = list(range(1, blocks))
    arrived = {slot: exchange(spectra, "inp", slot) for slot in reversed(slots)}
    early, late = slots[: CORES - 1], slots[CORES - 1 :]
    visibilities, left = pl.pallas_call(
        functools.partial(correlate_first, scale, blocks, [0] + early),
        in_specs=[smem, vmem, vmem] + [vmem] * len(early),
        out_specs=[hbm, vmem],
        out_shape=[out_shape, left_shape],
        scratch_shapes=scratch(1 + len(early), inputs),
        cost_estimate=pl.CostEstimate(flops=MIB << 7, bytes_accessed=2 * MIB, transcendentals=0),
        compiler_params=pltpu.CompilerParams(vmem_limit_bytes=16 * MIB),
        name="correlate_first",
    )(my_block, spectra, spectra, *[arrived[slot] for slot in early])
    return pl.pallas_call(
        functools.partial(correlate_rest, scale, blocks, late),
        in_specs=[smem, vmem] + [vmem] * len(late) + [hbm],
        out_specs=hbm,
        out_shape=out_shape,
        scratch_shapes=scratch(len(late), inputs),
        input_output_aliases={2 + len(late): 0},
        compiler_params=pltpu.CompilerParams(vmem_limit_bytes=16 * MIB),
        name="correlate_rest",
    )(my_block, left, *[arrived[slot] for slot in late], visibilities)


def solution(mesh):
    in_specs = (P(("grp", "tm"), "inp", None), P(), P(("grp", "tm"), "inp"))
    out_specs = P(("grp", "tm"), None, "inp", None)
    return jax.shard_map(shards, mesh=mesh, in_specs=in_specs, out_specs=out_specs, check_vma=False)
```

```python
import functools

import jax
import jax.numpy as jnp
import ml_dtypes
import numpy as np
from jax import lax
from jax.experimental import pallas as pl
from jax.experimental.pallas import tpu as pltpu
from jax.sharding import PartitionSpec as P

NCH = 4096
CH_DEV = 2
SUBLANES = 8
LANES = 128
CORES = 2
ROW_TILE = 16
FLAGGED = 1e30
MIB = 1 << 20
WIDTH = 1024
AHEAD = 2


def round_up(value, step):
    return -(-value // step) * step


def partner(index, distance, count):
    if count & (count - 1) == 0:
        return index ^ distance
    return (distance - index) % count


def exchange(value, axis, distance):
    count = lax.axis_size(axis)
    return lax.ppermute(value, axis, [(source, partner(source, distance, count)) for source in range(count)])


def slab_table(length, slabs, lowest):
    sample_ids = np.arange(length, dtype=np.int64)
    channel_ids = lowest + np.arange(slabs * CH_DEV, dtype=np.int64)
    angle = 2.0 * np.pi / length * (channel_ids[:, None] * sample_ids[None, :] % length)
    factor = np.sqrt(2.0 / length)
    both = np.stack([factor * np.cos(angle), -factor * np.sin(angle)], axis=0)
    by_slab = both.reshape(2, slabs, CH_DEV, length).transpose(1, 0, 2, 3).reshape(slabs, 2 * CH_DEV, length)
    return np.tile(by_slab, (1, SUBLANES // (2 * CH_DEV), 1)).astype(ml_dtypes.bfloat16)


def cut(length):
    widths = [WIDTH // 2] + [WIDTH] * (length // WIDTH - 1) + [WIDTH // 2] if length % WIDTH == 0 else [length]
    starts = np.cumsum([0] + widths)
    return [(int(start), width) for start, width in zip(starts, widths)]


def channelize(slabs, me_ref, samples_hbm, fir_hbm, table_hbm, flags_hbm, *rest):
    outs, (samples, fir, table, flags, weights, sums, total, chunk_sems, sems) = rest[:slabs], rest[slabs:]
    frames, inputs, length = samples.shape
    taps = fir.shape[0]
    group = 2 * CH_DEV
    per_slab = taps * group
    pack = SUBLANES // group
    chunks = cut(length)
    small = [
        pltpu.make_async_copy(source, target, sems.at[place])
        for place, (source, target) in enumerate(((fir_hbm, fir), (table_hbm, table), (flags_hbm, flags)))
    ]
    loads = [
        pltpu.make_async_copy(
            samples_hbm.at[:, :, pl.ds(start, width)], samples.at[:, :, pl.ds(start, width)], chunk_sems.at[place]
        )
        for place, (start, width) in enumerate(chunks)
    ]
    for copy in small + loads[:AHEAD]:
        copy.start()

    def make_weights(start, width):
        row_ids = lax.broadcasted_iota(jnp.int32, (SUBLANES, width), 0)
        columns = pl.ds(start, width)
        tables = [table[partner(me_ref[0], slot, slabs), :, columns].astype(jnp.float32) for slot in range(slabs)]
        for first in range(0, taps, 2 * pack):
            coefs = []
            for half in range(2):
                coef = None
                for place in range(pack):
                    tap = taps - 1 - (first + half * pack + place)
                    line = jnp.broadcast_to(fir[tap : tap + 1, columns], (SUBLANES, width))
                    coef = line if coef is None else jnp.where(row_ids >= place * group, line, coef)
                coefs.append(coef)
            for slot in range(slabs):
                rows = jnp.concatenate([coef * tables[slot] for coef in coefs], axis=0)
                weights[pl.ds(slot * per_slab + first * group, ROW_TILE), columns] = rows.astype(jnp.bfloat16)

    total[...] = jnp.zeros_like(total)
    for copy in small:
        copy.wait()
    for copy in loads[AHEAD:]:
        copy.start()
    make_weights(*chunks[0])
    for place, (start, width) in enumerate(chunks):
        loads[place].wait()
        columns = pl.ds(start, width)
        if place + 1 < len(chunks):
            make_weights(*chunks[place + 1])
        for frame in range(frames):
            before = sums[frame] if place else jnp.zeros(sums.shape[1:], jnp.float32)
            after = before + lax.dot_general(
                weights[:, columns],
                samples[frame, :, columns],
                (((1,), (1,)), ((), ())),
                preferred_element_type=jnp.float32,
            )
            if place + 1 < len(chunks):
                sums[frame] = after
                continue
            for slot in range(slabs):
                total[slot, pl.ds(frame * group, per_slab), :] += after[slot * per_slab : (slot + 1) * per_slab]

    good = jnp.broadcast_to(flags[...][:, None, :], (frames, group, inputs)).reshape(frames * group, inputs)
    own = frames * group
    for slot in range(slabs):
        total[slot, 0:own, :] = jnp.where(good == 0, FLAGGED, total[slot, 0:own, :])
        outs[slot][...] = total[slot].astype(outs[slot].dtype)


def add_hops(slabs, frames, me_ref, *rest):
    pieces, (out_ref, total) = rest[:slabs][::-1], rest[slabs:]
    group = 2 * CH_DEV
    total[...] = jnp.zeros_like(total)
    for slot in range(slabs):
        place = pl.multiple_of(partner(me_ref[0], slot, slabs) * (frames * group), SUBLANES)
        total[pl.ds(place, pieces[slot].shape[0]), :] += pieces[slot][...].astype(jnp.float32)
    value = total[0 : out_ref.shape[0], :]
    out_ref[...] = jnp.where(value > 0.5 * FLAGGED, 0.0, value).astype(out_ref.dtype)


def make_left(own_ref, left_ref):
    rows, inputs = own_ref.shape
    group = 2 * CH_DEV
    own = own_ref[...].astype(jnp.float32)
    row_ids = lax.broadcasted_iota(jnp.int32, own.shape, 0)
    is_real = row_ids % group < CH_DEV
    turned = jnp.where(is_real, pltpu.roll(own, rows - CH_DEV, 0), -pltpu.roll(own, CH_DEV, 0))
    for channel in range(CH_DEV):
        keep = row_ids % CH_DEV == channel
        for part, value in enumerate((own, turned)):
            place = (channel * 2 + part) * inputs
            left_ref[pl.ds(place, inputs), :] = jnp.where(keep, value, 0.0).T.astype(left_ref.dtype)


def multiply(scale, blocks, slots, me_ref, left_ref, pieces, out_hbm, parts, sems):
    copies = []
    inputs = parts.shape[3]
    for place, (slot, piece) in enumerate(zip(slots, pieces)):
        width = piece.shape[1]
        first = 0 if blocks == 1 else pl.multiple_of(partner(me_ref[0], slot, blocks) * width, LANES)
        for channel in range(CH_DEV):
            for part in range(2):
                rows = left_ref[pl.ds((channel * 2 + part) * inputs, inputs), :]
                parts[place, channel, part] = jnp.dot(rows, piece[...], preferred_element_type=jnp.float32) * scale
                copies.append(
                    pltpu.make_async_copy(
                        parts.at[place, channel, part],
                        out_hbm.at[channel, part, :, pl.ds(first, width)],
                        sems.at[place, channel, part],
                    )
                )
                copies[-1].start()
    for copy in copies:
        copy.wait()


def correlate_first(scale, blocks, slots, me_ref, own_ref, *rest):
    pieces, (out_hbm, left_ref, parts, sems) = rest[: len(slots)], rest[len(slots) :]
    make_left(own_ref, left_ref)
    multiply(scale, blocks, slots, me_ref, left_ref, pieces, out_hbm, parts, sems)


def correlate_rest(scale, blocks, slots, me_ref, left_ref, *rest):
    pieces, (_, out_hbm, parts, sems) = rest[: len(slots)], rest[len(slots) :]
    multiply(scale, blocks, slots, me_ref, left_ref, pieces, out_hbm, parts, sems)


def shards(samples, fir, flags):
    frames, inputs, length = samples.shape
    taps = fir.shape[0]
    slabs = lax.axis_size("tm")
    blocks = lax.axis_size("inp")
    group = 2 * CH_DEV
    window = frames + taps - 1
    rows = round_up(window * group, ROW_TILE)
    spectra_rows = slabs * frames * group
    table = jnp.asarray(slab_table(length, slabs, NCH // 4))
    my_slab = lax.axis_index("tm").astype(jnp.int32).reshape(1)
    my_block = lax.axis_index("inp").astype(jnp.int32).reshape(1)

    chunks = len(cut(length))
    sent = pl.pallas_call(
        functools.partial(channelize, slabs),
        in_specs=[pl.BlockSpec(memory_space=pltpu.SMEM)] + [pl.BlockSpec(memory_space=pltpu.HBM)] * 4,
        out_specs=[pl.BlockSpec(memory_space=pltpu.VMEM)] * slabs,
        scratch_shapes=[
            pltpu.VMEM(samples.shape, samples.dtype),
            pltpu.VMEM(fir.shape, fir.dtype),
            pltpu.VMEM(table.shape, table.dtype),
            pltpu.VMEM(flags.shape, flags.dtype),
            pltpu.VMEM((slabs * taps * group, length), jnp.bfloat16),
            pltpu.VMEM((frames, slabs * taps * group, inputs), jnp.float32),
            pltpu.VMEM((slabs, rows, inputs), jnp.float32),
            pltpu.SemaphoreType.DMA((chunks,)),
            pltpu.SemaphoreType.DMA((3,)),
        ],
        out_shape=[
            jax.ShapeDtypeStruct((rows, inputs), jnp.bfloat16 if slot else jnp.float32) for slot in range(slabs)
        ],
        compiler_params=pltpu.CompilerParams(vmem_limit_bytes=56 * MIB),
        name="channelize",
    )(my_slab, samples, fir, table, flags)

    arrived = {slot: exchange(sent[slot], "tm", slot) for slot in reversed(range(1, slabs))}
    pieces = [jnp.maximum(sent[0], -FLAGGED)] + [arrived[slot] for slot in range(1, slabs)]
    smem = pl.BlockSpec(memory_space=pltpu.SMEM)
    vmem = pl.BlockSpec(memory_space=pltpu.VMEM)
    hbm = pl.BlockSpec(memory_space=pltpu.HBM)
    spectra = pl.pallas_call(
        functools.partial(add_hops, slabs, frames),
        in_specs=[smem] + [vmem] * slabs,
        out_specs=vmem,
        scratch_shapes=[pltpu.VMEM((spectra_rows + rows, inputs), jnp.float32)],
        out_shape=jax.ShapeDtypeStruct((spectra_rows, inputs), jnp.bfloat16),
        compiler_params=pltpu.CompilerParams(vmem_limit_bytes=4 * MIB),
        name="add_hops",
    )(my_slab, *pieces[::-1])

    scale = 1.0 / (slabs * frames)
    out_shape = jax.ShapeDtypeStruct((CH_DEV, 2, inputs, blocks * inputs), jnp.float32)
    left_shape = jax.ShapeDtypeStruct((CH_DEV * 2 * inputs, spectra_rows), jnp.bfloat16)

    def scratch(count, width):
        return [pltpu.VMEM((count, CH_DEV, 2, inputs, width), jnp.float32), pltpu.SemaphoreType.DMA((count, CH_DEV, 2))]

    if inputs % LANES:
        columns = lax.all_gather(spectra, "inp", axis=1, tiled=True)
        return pl.pallas_call(
            functools.partial(correlate_first, scale, 1, (0,)),
            in_specs=[smem, vmem, vmem],
            out_specs=[hbm, vmem],
            out_shape=[out_shape, left_shape],
            scratch_shapes=scratch(1, blocks * inputs),
            compiler_params=pltpu.CompilerParams(vmem_limit_bytes=16 * MIB),
        name="correlate",
        )(my_block, spectra, columns)[0]

    slots = list(range(1, blocks))
    arrived = {slot: exchange(spectra, "inp", slot) for slot in reversed(slots)}
    early, late = slots[: CORES - 1], slots[CORES - 1 :]
    visibilities, left = pl.pallas_call(
        functools.partial(correlate_first, scale, blocks, [0] + early),
        in_specs=[smem, vmem, vmem] + [vmem] * len(early),
        out_specs=[hbm, vmem],
        out_shape=[out_shape, left_shape],
        scratch_shapes=scratch(1 + len(early), inputs),
        cost_estimate=pl.CostEstimate(flops=MIB << 7, bytes_accessed=2 * MIB, transcendentals=0),
        compiler_params=pltpu.CompilerParams(vmem_limit_bytes=16 * MIB),
        name="correlate_first",
    )(my_block, spectra, spectra, *[arrived[slot] for slot in early])
    for slot in reversed(late):
        visibilities = pl.pallas_call(
            functools.partial(correlate_rest, scale, blocks, [slot]),
            in_specs=[smem, vmem, vmem, hbm],
            out_specs=hbm,
            out_shape=out_shape,
            scratch_shapes=scratch(1, inputs),
            input_output_aliases={3: 0},
            compiler_params=pltpu.CompilerParams(vmem_limit_bytes=16 * MIB),
            name="correlate_rest",
        )(my_block, left, arrived[slot], visibilities)
    return visibilities


def solution(mesh):
    in_specs = (P(("grp", "tm"), "inp", None), P(), P(("grp", "tm"), "inp"))
    out_specs = P(("grp", "tm"), None, "inp", None)
    return jax.shard_map(shards, mesh=mesh, in_specs=in_specs, out_specs=out_specs, check_vma=False)
```

```python
import functools

import jax
import jax.numpy as jnp
import ml_dtypes
import numpy as np
from jax import lax
from jax.experimental import pallas as pl
from jax.experimental.pallas import tpu as pltpu
from jax.sharding import PartitionSpec as P

NCH = 4096
CH_DEV = 2
SUBLANES = 8
LANES = 128
CORES = 2
ROW_TILE = 16
FLAGGED = 1e30
MIB = 1 << 20
WIDTH = 1024
AHEAD = 2


def round_up(value, step):
    return -(-value // step) * step


def partner(index, distance, count):
    if count & (count - 1) == 0:
        return index ^ distance
    return (distance - index) % count


def routes(count):
    if count == 4:
        return [(0, 1, 2, 3), (1, 0, 3, 2), (3, 2, 0, 1), (2, 3, 1, 0)]
    return [tuple(partner(source, slot, count) for source in range(count)) for slot in range(count)]


def pick(values, index):
    result = jnp.int32(values[0])
    for place in range(1, len(values)):
        result = jnp.where(index == place, jnp.int32(values[place]), result)
    return result


def exchange(value, axis, distance):
    count = lax.axis_size(axis)
    return lax.ppermute(value, axis, [(source, partner(source, distance, count)) for source in range(count)])


def slab_table(length, slabs, lowest):
    sample_ids = np.arange(length, dtype=np.int64)
    channel_ids = lowest + np.arange(slabs * CH_DEV, dtype=np.int64)
    angle = 2.0 * np.pi / length * (channel_ids[:, None] * sample_ids[None, :] % length)
    factor = np.sqrt(2.0 / length)
    both = np.stack([factor * np.cos(angle), -factor * np.sin(angle)], axis=0)
    by_slab = both.reshape(2, slabs, CH_DEV, length).transpose(1, 0, 2, 3).reshape(slabs, 2 * CH_DEV, length)
    return np.tile(by_slab, (1, SUBLANES // (2 * CH_DEV), 1)).astype(ml_dtypes.bfloat16)


def cut(length):
    widths = [WIDTH // 2] + [WIDTH] * (length // WIDTH - 1) + [WIDTH // 2] if length % WIDTH == 0 else [length]
    starts = np.cumsum([0] + widths)
    return [(int(start), width) for start, width in zip(starts, widths)]


def channelize(slabs, me_ref, samples_hbm, fir_hbm, table_hbm, flags_hbm, *rest):
    outs, (samples, fir, table, flags, weights, sums, total, chunk_sems, sems) = rest[:slabs], rest[slabs:]
    frames, inputs, length = samples.shape
    taps = fir.shape[0]
    group = 2 * CH_DEV
    per_slab = taps * group
    pack = SUBLANES // group
    chunks = cut(length)
    targets = routes(slabs)
    small = [
        pltpu.make_async_copy(source, target, sems.at[place])
        for place, (source, target) in enumerate(((fir_hbm, fir), (table_hbm, table), (flags_hbm, flags)))
    ]
    loads = [
        pltpu.make_async_copy(
            samples_hbm.at[:, :, pl.ds(start, width)], samples.at[:, :, pl.ds(start, width)], chunk_sems.at[place]
        )
        for place, (start, width) in enumerate(chunks)
    ]
    for copy in small + loads[:AHEAD]:
        copy.start()

    def make_weights(start, width):
        row_ids = lax.broadcasted_iota(jnp.int32, (SUBLANES, width), 0)
        columns = pl.ds(start, width)
        tables = [table[pick(targets[slot], me_ref[0]), :, columns].astype(jnp.float32) for slot in range(slabs)]
        for first in range(0, taps, 2 * pack):
            coefs = []
            for half in range(2):
                coef = None
                for place in range(pack):
                    tap = taps - 1 - (first + half * pack + place)
                    line = jnp.broadcast_to(fir[tap : tap + 1, columns], (SUBLANES, width))
                    coef = line if coef is None else jnp.where(row_ids >= place * group, line, coef)
                coefs.append(coef)
            for slot in range(slabs):
                rows = jnp.concatenate([coef * tables[slot] for coef in coefs], axis=0)
                weights[pl.ds(slot * per_slab + first * group, ROW_TILE), columns] = rows.astype(jnp.bfloat16)

    total[...] = jnp.zeros_like(total)
    for copy in small:
        copy.wait()
    for copy in loads[AHEAD:]:
        copy.start()
    make_weights(*chunks[0])
    for place, (start, width) in enumerate(chunks):
        loads[place].wait()
        columns = pl.ds(start, width)
        if place + 1 < len(chunks):
            make_weights(*chunks[place + 1])
        for frame in range(frames):
            before = sums[frame] if place else jnp.zeros(sums.shape[1:], jnp.float32)
            after = before + lax.dot_general(
                weights[:, columns],
                samples[frame, :, columns],
                (((1,), (1,)), ((), ())),
                preferred_element_type=jnp.float32,
            )
            if place + 1 < len(chunks):
                sums[frame] = after
                continue
            for slot in range(slabs):
                total[slot, pl.ds(frame * group, per_slab), :] += after[slot * per_slab : (slot + 1) * per_slab]

    good = jnp.broadcast_to(flags[...][:, None, :], (frames, group, inputs)).reshape(frames * group, inputs)
    own = frames * group
    for slot in range(slabs):
        total[slot, 0:own, :] = jnp.where(good == 0, FLAGGED, total[slot, 0:own, :])
        outs[slot][...] = total[slot].astype(outs[slot].dtype)


def add_hops(slabs, frames, me_ref, *rest):
    pieces, (out_ref, total) = rest[:slabs][::-1], rest[slabs:]
    group = 2 * CH_DEV
    targets = routes(slabs)
    total[...] = jnp.zeros_like(total)
    for slot in range(slabs):
        source = pick([targets[slot].index(place) for place in range(slabs)], me_ref[0])
        place = pl.multiple_of(source * (frames * group), SUBLANES)
        total[pl.ds(place, pieces[slot].shape[0]), :] += pieces[slot][...].astype(jnp.float32)
    value = total[0 : out_ref.shape[0], :]
    out_ref[...] = jnp.where(value > 0.5 * FLAGGED, 0.0, value).astype(out_ref.dtype)


def make_left(own_ref, left_ref):
    rows, inputs = own_ref.shape
    group = 2 * CH_DEV
    own = own_ref[...].astype(jnp.float32)
    row_ids = lax.broadcasted_iota(jnp.int32, own.shape, 0)
    is_real = row_ids % group < CH_DEV
    turned = jnp.where(is_real, pltpu.roll(own, rows - CH_DEV, 0), -pltpu.roll(own, CH_DEV, 0))
    for channel in range(CH_DEV):
        keep = row_ids % CH_DEV == channel
        for part, value in enumerate((own, turned)):
            place = (channel * 2 + part) * inputs
            left_ref[pl.ds(place, inputs), :] = jnp.where(keep, value, 0.0).T.astype(left_ref.dtype)


def multiply(scale, blocks, slots, me_ref, left_ref, pieces, out_hbm, parts, sems):
    copies = []
    inputs = parts.shape[3]
    for place, (slot, piece) in enumerate(zip(slots, pieces)):
        width = piece.shape[1]
        first = 0 if blocks == 1 else pl.multiple_of(partner(me_ref[0], slot, blocks) * width, LANES)
        for channel in range(CH_DEV):
            for part in range(2):
                rows = left_ref[pl.ds((channel * 2 + part) * inputs, inputs), :]
                parts[place, channel, part] = jnp.dot(rows, piece[...], preferred_element_type=jnp.float32) * scale
                copies.append(
                    pltpu.make_async_copy(
                        parts.at[place, channel, part],
                        out_hbm.at[channel, part, :, pl.ds(first, width)],
                        sems.at[place, channel, part],
                    )
                )
                copies[-1].start()
    for copy in copies:
        copy.wait()


def correlate_first(scale, blocks, slots, me_ref, own_ref, *rest):
    pieces, (out_hbm, left_ref, parts, sems) = rest[: len(slots)], rest[len(slots) :]
    make_left(own_ref, left_ref)
    multiply(scale, blocks, slots, me_ref, left_ref, pieces, out_hbm, parts, sems)


def correlate_rest(scale, blocks, slots, me_ref, left_ref, *rest):
    pieces, (_, out_hbm, parts, sems) = rest[: len(slots)], rest[len(slots) :]
    multiply(scale, blocks, slots, me_ref, left_ref, pieces, out_hbm, parts, sems)


def shards(samples, fir, flags):
    frames, inputs, length = samples.shape
    taps = fir.shape[0]
    slabs = lax.axis_size("tm")
    blocks = lax.axis_size("inp")
    group = 2 * CH_DEV
    window = frames + taps - 1
    rows = round_up(window * group, ROW_TILE)
    spectra_rows = slabs * frames * group
    table = jnp.asarray(slab_table(length, slabs, NCH // 4))
    my_slab = lax.axis_index("tm").astype(jnp.int32).reshape(1)
    my_block = lax.axis_index("inp").astype(jnp.int32).reshape(1)

    chunks = len(cut(length))
    sent = pl.pallas_call(
        functools.partial(channelize, slabs),
        in_specs=[pl.BlockSpec(memory_space=pltpu.SMEM)] + [pl.BlockSpec(memory_space=pltpu.HBM)] * 4,
        out_specs=[pl.BlockSpec(memory_space=pltpu.VMEM)] * slabs,
        scratch_shapes=[
            pltpu.VMEM(samples.shape, samples.dtype),
            pltpu.VMEM(fir.shape, fir.dtype),
            pltpu.VMEM(table.shape, table.dtype),
            pltpu.VMEM(flags.shape, flags.dtype),
            pltpu.VMEM((slabs * taps * group, length), jnp.bfloat16),
            pltpu.VMEM((frames, slabs * taps * group, inputs), jnp.float32),
            pltpu.VMEM((slabs, rows, inputs), jnp.float32),
            pltpu.SemaphoreType.DMA((chunks,)),
            pltpu.SemaphoreType.DMA((3,)),
        ],
        out_shape=[
            jax.ShapeDtypeStruct((rows, inputs), jnp.bfloat16 if slot else jnp.float32) for slot in range(slabs)
        ],
        compiler_params=pltpu.CompilerParams(vmem_limit_bytes=56 * MIB),
        name="channelize",
    )(my_slab, samples, fir, table, flags)

    arrived = {
        slot: lax.ppermute(sent[slot], "tm", list(enumerate(routes(slabs)[slot]))) for slot in reversed(range(1, slabs))
    }
    pieces = [jnp.maximum(sent[0], -FLAGGED)] + [arrived[slot] for slot in range(1, slabs)]
    smem = pl.BlockSpec(memory_space=pltpu.SMEM)
    vmem = pl.BlockSpec(memory_space=pltpu.VMEM)
    hbm = pl.BlockSpec(memory_space=pltpu.HBM)
    spectra = pl.pallas_call(
        functools.partial(add_hops, slabs, frames),
        in_specs=[smem] + [vmem] * slabs,
        out_specs=vmem,
        scratch_shapes=[pltpu.VMEM((spectra_rows + rows, inputs), jnp.float32)],
        out_shape=jax.ShapeDtypeStruct((spectra_rows, inputs), jnp.bfloat16),
        compiler_params=pltpu.CompilerParams(vmem_limit_bytes=4 * MIB),
        name="add_hops",
    )(my_slab, *pieces[::-1])

    scale = 1.0 / (slabs * frames)
    out_shape = jax.ShapeDtypeStruct((CH_DEV, 2, inputs, blocks * inputs), jnp.float32)
    left_shape = jax.ShapeDtypeStruct((CH_DEV * 2 * inputs, spectra_rows), jnp.bfloat16)

    def scratch(count, width):
        return [pltpu.VMEM((count, CH_DEV, 2, inputs, width), jnp.float32), pltpu.SemaphoreType.DMA((count, CH_DEV, 2))]

    if inputs % LANES:
        columns = lax.all_gather(spectra, "inp", axis=1, tiled=True)
        return pl.pallas_call(
            functools.partial(correlate_first, scale, 1, (0,)),
            in_specs=[smem, vmem, vmem],
            out_specs=[hbm, vmem],
            out_shape=[out_shape, left_shape],
            scratch_shapes=scratch(1, blocks * inputs),
            compiler_params=pltpu.CompilerParams(vmem_limit_bytes=16 * MIB),
        name="correlate",
        )(my_block, spectra, columns)[0]

    slots = list(range(1, blocks))
    arrived = {slot: exchange(spectra, "inp", slot) for slot in reversed(slots)}
    early, late = slots[: CORES - 1], slots[CORES - 1 :]
    visibilities, left = pl.pallas_call(
        functools.partial(correlate_first, scale, blocks, [0] + early),
        in_specs=[smem, vmem, vmem] + [vmem] * len(early),
        out_specs=[hbm, vmem],
        out_shape=[out_shape, left_shape],
        scratch_shapes=scratch(1 + len(early), inputs),
        cost_estimate=pl.CostEstimate(flops=MIB << 7, bytes_accessed=2 * MIB, transcendentals=0),
        compiler_params=pltpu.CompilerParams(vmem_limit_bytes=16 * MIB),
        name="correlate_first",
    )(my_block, spectra, spectra, *[arrived[slot] for slot in early])
    for slot in reversed(late):
        visibilities = pl.pallas_call(
            functools.partial(correlate_rest, scale, blocks, [slot]),
            in_specs=[smem, vmem, vmem, hbm],
            out_specs=hbm,
            out_shape=out_shape,
            scratch_shapes=scratch(1, inputs),
            input_output_aliases={3: 0},
            compiler_params=pltpu.CompilerParams(vmem_limit_bytes=16 * MIB),
            name="correlate_rest",
        )(my_block, left, arrived[slot], visibilities)
    return visibilities


def solution(mesh):
    in_specs = (P(("grp", "tm"), "inp", None), P(), P(("grp", "tm"), "inp"))
    out_specs = P(("grp", "tm"), None, "inp", None)
    return jax.shard_map(shards, mesh=mesh, in_specs=in_specs, out_specs=out_specs, check_vma=False)
```

```python
import functools

import jax
import jax.numpy as jnp
import ml_dtypes
import numpy as np
from jax import lax
from jax.experimental import pallas as pl
from jax.experimental.pallas import tpu as pltpu
from jax.sharding import PartitionSpec as P

NCH = 4096
CH_DEV = 2
SUBLANES = 8
LANES = 128
CORES = 2
ROW_TILE = 16
FLAGGED = 1e30
MIB = 1 << 20
WIDTH = 1024
AHEAD = 2


def round_up(value, step):
    return -(-value // step) * step


def partner(index, distance, count):
    if count & (count - 1) == 0:
        return index ^ distance
    return (distance - index) % count


def routes(count):
    if count == 4:
        return [(0, 1, 2, 3), (1, 0, 3, 2), (3, 2, 0, 1), (2, 3, 1, 0)]
    return [tuple(partner(source, slot, count) for source in range(count)) for slot in range(count)]


def pick(values, index):
    result = jnp.int32(values[0])
    for place in range(1, len(values)):
        result = jnp.where(index == place, jnp.int32(values[place]), result)
    return result


def exchange(value, axis, distance):
    count = lax.axis_size(axis)
    return lax.ppermute(value, axis, [(source, partner(source, distance, count)) for source in range(count)])


def slab_table(length, slabs, lowest):
    sample_ids = np.arange(length, dtype=np.int64)
    channel_ids = lowest + np.arange(slabs * CH_DEV, dtype=np.int64)
    angle = 2.0 * np.pi / length * (channel_ids[:, None] * sample_ids[None, :] % length)
    factor = np.sqrt(2.0 / length)
    both = np.stack([factor * np.cos(angle), -factor * np.sin(angle)], axis=0)
    by_slab = both.reshape(2, slabs, CH_DEV, length).transpose(1, 0, 2, 3).reshape(slabs, 2 * CH_DEV, length)
    return np.tile(by_slab, (1, SUBLANES // (2 * CH_DEV), 1)).astype(ml_dtypes.bfloat16)


def cut(length):
    widths = [WIDTH // 2] + [WIDTH] * (length // WIDTH - 1) + [WIDTH // 2] if length % WIDTH == 0 else [length]
    starts = np.cumsum([0] + widths)
    return [(int(start), width) for start, width in zip(starts, widths)]


def channelize(slabs, me_ref, samples_hbm, fir_hbm, table_hbm, flags_hbm, *rest):
    outs, (samples, fir, table, flags, weights, sums, total, chunk_sems, sems) = rest[:slabs], rest[slabs:]
    frames, inputs, length = samples.shape
    taps = fir.shape[0]
    group = 2 * CH_DEV
    per_slab = taps * group
    pack = SUBLANES // group
    chunks = cut(length)
    targets = routes(slabs)
    small = [
        pltpu.make_async_copy(source, target, sems.at[place])
        for place, (source, target) in enumerate(((fir_hbm, fir), (table_hbm, table), (flags_hbm, flags)))
    ]
    loads = [
        pltpu.make_async_copy(
            samples_hbm.at[:, :, pl.ds(start, width)], samples.at[:, :, pl.ds(start, width)], chunk_sems.at[place]
        )
        for place, (start, width) in enumerate(chunks)
    ]
    for copy in small + loads[:AHEAD]:
        copy.start()

    def make_weights(start, width):
        row_ids = lax.broadcasted_iota(jnp.int32, (SUBLANES, width), 0)
        columns = pl.ds(start, width)
        tables = [table[pick(targets[slot], me_ref[0]), :, columns].astype(jnp.float32) for slot in range(slabs)]
        for first in range(0, taps, 2 * pack):
            coefs = []
            for half in range(2):
                coef = None
                for place in range(pack):
                    tap = taps - 1 - (first + half * pack + place)
                    line = jnp.broadcast_to(fir[tap : tap + 1, columns], (SUBLANES, width))
                    coef = line if coef is None else jnp.where(row_ids >= place * group, line, coef)
                coefs.append(coef)
            for slot in range(slabs):
                rows = jnp.concatenate([coef * tables[slot] for coef in coefs], axis=0)
                weights[pl.ds(slot * per_slab + first * group, ROW_TILE), columns] = rows.astype(jnp.bfloat16)

    total[...] = jnp.zeros_like(total)
    for copy in small:
        copy.wait()
    for copy in loads[AHEAD:]:
        copy.start()
    make_weights(*chunks[0])
    for place, (start, width) in enumerate(chunks):
        loads[place].wait()
        columns = pl.ds(start, width)
        if place + 1 < len(chunks):
            make_weights(*chunks[place + 1])
        for frame in range(frames):
            before = sums[frame] if place else jnp.zeros(sums.shape[1:], jnp.float32)
            after = before + lax.dot_general(
                weights[:, columns],
                samples[frame, :, columns],
                (((1,), (1,)), ((), ())),
                preferred_element_type=jnp.float32,
            )
            if place + 1 < len(chunks):
                sums[frame] = after
                continue
            for slot in range(slabs):
                total[slot, pl.ds(frame * group, per_slab), :] += after[slot * per_slab : (slot + 1) * per_slab]

    good = jnp.broadcast_to(flags[...][:, None, :], (frames, group, inputs)).reshape(frames * group, inputs)
    own = frames * group
    for slot in range(slabs):
        total[slot, 0:own, :] = jnp.where(good == 0, FLAGGED, total[slot, 0:own, :])
        outs[slot][...] = total[slot].astype(outs[slot].dtype)


def add_hops(slabs, frames, me_ref, *rest):
    pieces, (out_ref, total) = rest[:slabs][::-1], rest[slabs:]
    group = 2 * CH_DEV
    targets = routes(slabs)
    total[...] = jnp.zeros_like(total)
    for slot in range(slabs):
        source = pick([targets[slot].index(place) for place in range(slabs)], me_ref[0])
        place = pl.multiple_of(source * (frames * group), SUBLANES)
        total[pl.ds(place, pieces[slot].shape[0]), :] += pieces[slot][...].astype(jnp.float32)
    value = total[0 : out_ref.shape[0], :]
    out_ref[...] = jnp.where(value > 0.5 * FLAGGED, 0.0, value).astype(out_ref.dtype)


def make_left(own_ref, left_ref):
    rows, inputs = own_ref.shape
    group = 2 * CH_DEV
    own = own_ref[...].astype(jnp.float32)
    row_ids = lax.broadcasted_iota(jnp.int32, own.shape, 0)
    is_real = row_ids % group < CH_DEV
    turned = jnp.where(is_real, pltpu.roll(own, rows - CH_DEV, 0), -pltpu.roll(own, CH_DEV, 0))
    for channel in range(CH_DEV):
        keep = row_ids % CH_DEV == channel
        for part, value in enumerate((own, turned)):
            place = (channel * 2 + part) * inputs
            left_ref[pl.ds(place, inputs), :] = jnp.where(keep, value, 0.0).T.astype(left_ref.dtype)


def multiply(scale, blocks, slots, me_ref, left_ref, pieces, out_hbm, parts, sems):
    copies = []
    inputs = parts.shape[3]
    for place, (slot, piece) in enumerate(zip(slots, pieces)):
        width = piece.shape[1]
        first = 0 if blocks == 1 else pl.multiple_of(partner(me_ref[0], slot, blocks) * width, LANES)
        for channel in range(CH_DEV):
            for part in range(2):
                rows = left_ref[pl.ds((channel * 2 + part) * inputs, inputs), :]
                parts[place, channel, part] = jnp.dot(rows, piece[...], preferred_element_type=jnp.float32) * scale
                copies.append(
                    pltpu.make_async_copy(
                        parts.at[place, channel, part],
                        out_hbm.at[channel, part, :, pl.ds(first, width)],
                        sems.at[place, channel, part],
                    )
                )
                copies[-1].start()
    for copy in copies:
        copy.wait()


def correlate_first(scale, blocks, slots, me_ref, own_ref, *rest):
    pieces, (out_hbm, left_ref, parts, sems) = rest[: len(slots)], rest[len(slots) :]
    make_left(own_ref, left_ref)
    multiply(scale, blocks, slots, me_ref, left_ref, pieces, out_hbm, parts, sems)


def correlate_rest(scale, blocks, slots, me_ref, left_ref, *rest):
    pieces, (_, out_hbm, parts, sems) = rest[: len(slots)], rest[len(slots) :]
    multiply(scale, blocks, slots, me_ref, left_ref, pieces, out_hbm, parts, sems)


def shards(samples, fir, flags):
    frames, inputs, length = samples.shape
    taps = fir.shape[0]
    slabs = lax.axis_size("tm")
    blocks = lax.axis_size("inp")
    group = 2 * CH_DEV
    window = frames + taps - 1
    rows = round_up(window * group, ROW_TILE)
    spectra_rows = slabs * frames * group
    table = jnp.asarray(slab_table(length, slabs, NCH // 4))
    my_slab = lax.axis_index("tm").astype(jnp.int32).reshape(1)
    my_block = lax.axis_index("inp").astype(jnp.int32).reshape(1)

    chunks = len(cut(length))
    sent = pl.pallas_call(
        functools.partial(channelize, slabs),
        in_specs=[pl.BlockSpec(memory_space=pltpu.SMEM)] + [pl.BlockSpec(memory_space=pltpu.HBM)] * 4,
        out_specs=[pl.BlockSpec(memory_space=pltpu.VMEM)] * slabs,
        scratch_shapes=[
            pltpu.VMEM(samples.shape, samples.dtype),
            pltpu.VMEM(fir.shape, fir.dtype),
            pltpu.VMEM(table.shape, table.dtype),
            pltpu.VMEM(flags.shape, flags.dtype),
            pltpu.VMEM((slabs * taps * group, length), jnp.bfloat16),
            pltpu.VMEM((frames, slabs * taps * group, inputs), jnp.float32),
            pltpu.VMEM((slabs, rows, inputs), jnp.float32),
            pltpu.SemaphoreType.DMA((chunks,)),
            pltpu.SemaphoreType.DMA((3,)),
        ],
        out_shape=[
            jax.ShapeDtypeStruct((rows, inputs), jnp.bfloat16 if slot else jnp.float32) for slot in range(slabs)
        ],
        compiler_params=pltpu.CompilerParams(vmem_limit_bytes=56 * MIB),
        name="channelize",
    )(my_slab, samples, fir, table, flags)

    arrived = {
        slot: lax.ppermute(sent[slot], "tm", list(enumerate(routes(slabs)[slot]))) for slot in reversed(range(1, slabs))
    }
    pieces = [jnp.maximum(sent[0], -FLAGGED)] + [arrived[slot] for slot in range(1, slabs)]
    smem = pl.BlockSpec(memory_space=pltpu.SMEM)
    vmem = pl.BlockSpec(memory_space=pltpu.VMEM)
    hbm = pl.BlockSpec(memory_space=pltpu.HBM)
    spectra = pl.pallas_call(
        functools.partial(add_hops, slabs, frames),
        in_specs=[smem] + [vmem] * slabs,
        out_specs=vmem,
        scratch_shapes=[pltpu.VMEM((spectra_rows + rows, inputs), jnp.float32)],
        out_shape=jax.ShapeDtypeStruct((spectra_rows, inputs), jnp.bfloat16),
        compiler_params=pltpu.CompilerParams(vmem_limit_bytes=4 * MIB),
        name="add_hops",
    )(my_slab, *pieces[::-1])

    scale = 1.0 / (slabs * frames)
    out_shape = jax.ShapeDtypeStruct((CH_DEV, 2, inputs, blocks * inputs), jnp.float32)
    left_shape = jax.ShapeDtypeStruct((CH_DEV * 2 * inputs, spectra_rows), jnp.bfloat16)

    def scratch(count, width):
        return [pltpu.VMEM((count, CH_DEV, 2, inputs, width), jnp.float32), pltpu.SemaphoreType.DMA((count, CH_DEV, 2))]

    if inputs % LANES:
        columns = lax.all_gather(spectra, "inp", axis=1, tiled=True)
        return pl.pallas_call(
            functools.partial(correlate_first, scale, 1, (0,)),
            in_specs=[smem, vmem, vmem],
            out_specs=[hbm, vmem],
            out_shape=[out_shape, left_shape],
            scratch_shapes=scratch(1, blocks * inputs),
            compiler_params=pltpu.CompilerParams(vmem_limit_bytes=16 * MIB),
        name="correlate",
        )(my_block, spectra, columns)[0]

    slots = list(range(1, blocks))
    arrived = {slot: exchange(spectra, "inp", slot) for slot in reversed(slots)}
    early, late = slots[: CORES - 1], slots[CORES - 1 :]
    visibilities, left = pl.pallas_call(
        functools.partial(correlate_first, scale, blocks, [0] + early),
        in_specs=[smem, vmem, vmem] + [vmem] * len(early),
        out_specs=[hbm, vmem],
        out_shape=[out_shape, left_shape],
        scratch_shapes=scratch(1 + len(early), inputs),
        cost_estimate=pl.CostEstimate(flops=MIB << 7, bytes_accessed=2 * MIB, transcendentals=0),
        compiler_params=pltpu.CompilerParams(vmem_limit_bytes=16 * MIB),
        name="correlate_first",
    )(my_block, spectra, spectra, *[arrived[slot] for slot in early])
    for slot in late:
        visibilities = pl.pallas_call(
            functools.partial(correlate_rest, scale, blocks, [slot]),
            in_specs=[smem, vmem, vmem, hbm],
            out_specs=hbm,
            out_shape=out_shape,
            scratch_shapes=scratch(1, inputs),
            input_output_aliases={3: 0},
            compiler_params=pltpu.CompilerParams(vmem_limit_bytes=16 * MIB),
            name="correlate_rest",
        )(my_block, left, arrived[slot], visibilities)
    return visibilities


def solution(mesh):
    in_specs = (P(("grp", "tm"), "inp", None), P(), P(("grp", "tm"), "inp"))
    out_specs = P(("grp", "tm"), None, "inp", None)
    return jax.shard_map(shards, mesh=mesh, in_specs=in_specs, out_specs=out_specs, check_vma=False)
```
